32 devices in a mesh: fsdp: 4 (over x, core), dp: 8 (over z, y).
Axes of the slice: x: 2, y: 2, z: 4, core: 2. Of those that a mesh axis runs over, the one named last changes fastest.
Arguments:
- tokens: bfloat16 [16384, 768], P(('fsdp', 'dp')), may hold values from -6 to 6
- cotangent: bfloat16 [16384, 768], P(('fsdp', 'dp')), may hold values from -6 to 6
- seq_lengths: int32 [32, 2], P(('fsdp', 'dp')), may hold values from 0 to 512, as said below
- routes: int32 [16384, 1], P(('fsdp', 'dp')), may hold values from 0 to 7; in each aligned block of 512 rows (0 to 511, 512 to 1023, ...) at most 128 rows name the same one
- bucket_table: int32 [1024], replicated, may hold values from 0 to 31, as said below
- w_query: bfloat16 [768, 768], P('fsdp'), may hold values from -0.109375 to 0.109375
- w_key: bfloat16 [768, 768], P('fsdp'), may hold values from -0.109375 to 0.109375
- w_value: bfloat16 [768, 768], P('fsdp'), may hold values from -0.21875 to 0.21875
- w_output: bfloat16 [768, 768], P('fsdp'), may hold values from -0.875 to 0.875
- w_router: bfloat16 [768, 8], P('fsdp'), may hold values from -0.15625 to 0.15625
- norm_attn: bfloat16 [768], P('fsdp'), may hold values from 0.5 to 1.5
- norm_ffn: bfloat16 [768], P('fsdp'), may hold values from 0.5 to 1.5
- rel_bias: bfloat16 [32, 12], P('fsdp'), may hold values from -4 to 4
- expert_in: bfloat16 [8, 768, 3072], P('dp', None, 'fsdp'), may hold values from -0.21875 to 0.21875
- expert_out: bfloat16 [8, 3072, 768], P('dp', 'fsdp'), may hold values from -0.875 to 0.875
Outputs:
- layer_out: bfloat16 [16384, 768], P(('fsdp', 'dp'))
- grad_tokens: bfloat16 [16384, 768], P(('fsdp', 'dp'))
- grad_query: float32 [768, 768], P('fsdp')
- grad_key: float32 [768, 768], P('fsdp')
- grad_value: float32 [768, 768], P('fsdp')
- grad_output: float32 [768, 768], P('fsdp')
- grad_router: float32 [768, 8], P('fsdp')
- grad_norm_attn: float32 [768], P('fsdp')
- grad_norm_ffn: float32 [768], P('fsdp')
- grad_rel_bias: float32 [32, 12], P('fsdp')
- grad_expert_in: float32 [8, 768, 3072], P('dp', None, 'fsdp')
- grad_expert_out: float32 [8, 3072, 768], P('dp', 'fsdp')
The draws below stay inside these ranges and needn't reach their ends.
Inputs may be any that keep to these rules, and one draw needn't show every extreme that they name: `seq_lengths`: each row's lengths sum to 256 or more and at most 512; some row holds one sequence of 512. `routes`: no expert is named more than 128 times among the rows of one device, and in every draw some device names one expert exactly 128 times. `bucket_table`: entry 512 + j holds the bucket of offset j (key place minus query place); entry 0 is not read.
All inputs are finite; a program needn't handle non-finite values.
Results may differ from the reference program's by a relative error of at most 0.018.
Values may be sent and summed in bfloat16 or wider, within the bound.
A program may use at most 192 MiB of HBM per device.

```python
import math
import jax
import jax.numpy as jnp
import numpy as np
from jax import lax

D = 768
HEADS = 12
HEAD_DIM = 64
FF = 3072
BUCKETS = 32
TOK_DEV = 512
SEQ_DEV = 2
RANKS = 32
EXPERTS = 8
CAP = 128
TOKENS = 16384


def draw_seq_lengths(key, part):
    key = jax.random.fold_in(key, 11)
    key_total, key_full, key_cuts = jax.random.split(key, 3)
    totals = jax.random.randint(key_total, (RANKS,), TOK_DEV // 2, TOK_DEV + 1)
    full_rank = jax.random.randint(key_full, (), 0, RANKS)
    rank_ids = jnp.arange(RANKS, dtype=jnp.int32)
    totals = jnp.where(rank_ids == full_rank, TOK_DEV, totals).astype(jnp.int32)
    cut_points = jax.random.randint(key_cuts, (RANKS, SEQ_DEV - 1), 0, TOK_DEV + 1)
    cut_points = jnp.minimum(cut_points, totals[:, None])
    cut_points = jnp.where((rank_ids == full_rank)[:, None], TOK_DEV, cut_points)
    cut_points = jnp.sort(cut_points, axis=1).astype(jnp.int32)
    edge_points = jnp.concatenate([jnp.zeros((RANKS, 1), jnp.int32), cut_points, totals[:, None]], axis=1)
    return (edge_points[:, 1:] - edge_points[:, :-1]).astype(jnp.int32)


def draw_bucket_table(key, part):
    key = jax.random.fold_in(key, 23)
    half_count = BUCKETS // 2
    exact_count = half_count // 2
    bound_pool = jax.random.permutation(key, TOK_DEV - exact_count - 1)[:half_count - exact_count - 1] + exact_count + 1
    offset = jnp.arange(2 * TOK_DEV, dtype=jnp.int32) - TOK_DEV
    distance = jnp.abs(offset)
    counted = jnp.sum((distance[:, None] >= bound_pool[None, :]).astype(jnp.int32), axis=1)
    bucket = jnp.where(distance < exact_count, distance, exact_count + counted)
    return (bucket + half_count * (offset > 0).astype(jnp.int32)).astype(jnp.int32)


def block_scale(key, dims, pieces, smallest, largest):
    level = 1.0
    for dim, blocks in pieces:
        draws = jax.random.uniform(jax.random.fold_in(jax.random.fold_in(key, 6), dim), (blocks,), jnp.float32, smallest / len(pieces), largest / len(pieces))
        level = level * jnp.repeat(jnp.exp(draws), dims[dim] // blocks).reshape((-1,) + (1,) * (len(dims) - 1 - dim))
    return level


def shared_out(rng, own, number, rows, count, top, limit, skew):
    order = jax.random.permutation(rng, count)
    packed, common = shares(count, rows * top, limit, skew, True), shares(count, rows * top, limit, skew, False)
    places = jnp.arange(count)

    def named(lengths, rotation):
        used = int((lengths > 0).sum())
        fixed = max(1, used // 4)
        shifted = fixed + (places - fixed + rotation * (used - fixed)) % max(1, count - fixed)
        return jnp.zeros((count,), jnp.int32).at[order[jnp.where(places < fixed, places, shifted)]].set(jnp.asarray(lengths, jnp.int32))

    lengths = jnp.where(number % 4 == 0, named(packed, number // 4), named(common, number - number // 4 - 1))
    mixed = jax.random.permutation(jax.random.fold_in(own, 3), count)
    giver, taker = mixed[0:count // 2 * 2:2], mixed[1:count // 2 * 2:2]
    room = jnp.minimum(lengths[giver] - 1, limit - lengths[taker]) // 2
    room = jnp.where((giver == order[0]) | (taker == order[0]) | (lengths[taker] == 0), 0, jnp.maximum(room, 0))
    shifted = jax.random.randint(jax.random.fold_in(own, 4), (count // 2,), 0, 1 << 20) % (room + 1)
    lengths = lengths.at[giver].add(-shifted).at[taker].add(shifted)
    items = jnp.searchsorted(jnp.cumsum(lengths), jnp.arange(rows * top), side="right").astype(jnp.int32)
    table = items.reshape(top, rows).T
    table = table[jax.random.permutation(jax.random.fold_in(own, 1), rows)]
    rotation = jax.random.randint(jax.random.fold_in(own, 2), (rows, 1), 0, top)
    return jnp.take_along_axis(table, (jnp.arange(top)[None, :] + rotation) % top, axis=1)


def shares(amount, total, reach, skew, full):
    portions = [(1 << 20) // math.isqrt(grade ** skew) + 1 for grade in range(1, amount + 1)]
    largest = reach if full else min(reach, max(-(-total // amount), total * portions[0] // sum(portions)))
    least = 1 if total - largest >= amount - 1 else 0
    counts, spare = [largest] + [least] * (amount - 1), total - largest - least * (amount - 1)
    while spare > 0:
        free = [i for i in range(1, amount) if counts[i] < largest] or [i for i in range(1, amount) if counts[i] < reach]
        whole, left = sum([portions[i] for i in free]), spare
        for i in free:
            addition = min(reach - counts[i], max(1, left * portions[i] // whole), spare)
            counts[i] = counts[i] + addition
            spare = spare - addition
    return np.array(counts)


def gaussian(rng, extent, spread, reach, cuts=(), kind=jnp.bfloat16):
    loudness = block_scale(rng, extent, cuts, -0.22, 0.18) if cuts else 1.0
    entries = jax.random.normal(rng, extent, jnp.float32) * spread * loudness
    return jnp.minimum(jnp.maximum(entries, -reach), reach).astype(kind)


def setup_inputs(seed: int = 0) -> dict:
    key_list = jax.random.split(jax.random.key(seed), 16)
    tokens = gaussian(key_list[0], (TOKENS, D), 1.0, 6.0, ((0, 32),))
    cotangent = gaussian(key_list[1], (TOKENS, D), 1.0, 6.0, ((0, 32),))
    seq_lengths = draw_seq_lengths(jax.random.fold_in(key_list[15], 71), 0)
    routes_keys = jax.random.split(jax.random.fold_in(key_list[3], 1), TOKENS // TOK_DEV)
    routes_turns = jax.random.permutation(jax.random.fold_in(key_list[3], 3), TOKENS // TOK_DEV)
    routes = jax.vmap(lambda own, number: shared_out(jax.random.fold_in(key_list[3], 2), own, number, TOK_DEV, EXPERTS, 1, CAP, 2))(routes_keys, routes_turns).reshape((TOKENS, 1))
    bucket_table = draw_bucket_table(jax.random.fold_in(key_list[15], 71), 0)
    w_query = gaussian(key_list[5], (D, HEADS * HEAD_DIM), (4 * D) ** -0.5, 0.109375, ((0, 4),))
    w_key = gaussian(key_list[6], (D, HEADS * HEAD_DIM), (4 * D) ** -0.5, 0.109375, ((0, 4),))
    w_value = gaussian(key_list[7], (D, HEADS * HEAD_DIM), D ** -0.5, 0.21875, ((0, 4),))
    w_output = gaussian(key_list[8], (HEADS * HEAD_DIM, D), (HEADS * HEAD_DIM // 16) ** -0.5, 0.875, ((0, 4),))
    w_router = gaussian(key_list[9], (D, EXPERTS), (2 * D) ** -0.5, 0.15625, ((0, 4),))
    norm_attn = jnp.clip(1.0 + 0.1 * jax.random.normal(key_list[10], (D,), jnp.float32), 0.5, 1.5).astype(jnp.bfloat16)
    norm_ffn = jnp.clip(1.0 + 0.1 * jax.random.normal(key_list[11], (D,), jnp.float32), 0.5, 1.5).astype(jnp.bfloat16)
    rel_bias = gaussian(key_list[12], (BUCKETS, HEADS), 1.0, 4.0, ((0, 4),))
    expert_in = gaussian(key_list[13], (EXPERTS, D, FF), D ** -0.5, 0.21875, ((0, 8), (2, 4)))
    expert_out = gaussian(key_list[14], (EXPERTS, FF, D), (max(1, FF // (EXPERTS * EXPERTS))) ** -0.5, 0.875, ((0, 8), (1, 4)))
    return dict(tokens=tokens, cotangent=cotangent, seq_lengths=seq_lengths, routes=routes, bucket_table=bucket_table, w_query=w_query, w_key=w_key, w_value=w_value, w_output=w_output, w_router=w_router, norm_attn=norm_attn, norm_ffn=norm_ffn, rel_bias=rel_bias, expert_in=expert_in, expert_out=expert_out)


EPSILON = 1e-06
PRECISE = lax.Precision.HIGHEST
MASKED = -1e+30

@jax.custom_vjp
def low(v):
    return lax.optimization_barrier(v.astype(jnp.bfloat16)).astype(jnp.float32)

@jax.custom_vjp
def low_back(v):
    return v

def low_keep(v):
    return (low(v), None)

def low_pass(kept, grad):
    return (grad,)

def back_keep(v):
    return (v, None)

def back_low(kept, grad):
    return (low(grad),)
low.defvjp(low_keep, low_pass)
low_back.defvjp(back_keep, back_low)

def rms_norm(values, gain_vec):
    return values * lax.rsqrt(lax.optimization_barrier(jnp.mean(values * values, axis=-1, keepdims=True)) + EPSILON) * gain_vec

def segment_table(seq_lengths, tok_rows):
    ends_at = jnp.cumsum(seq_lengths, axis=-1).astype(jnp.int32)
    position = jnp.arange(tok_rows, dtype=jnp.int32)
    return lax.optimization_barrier(jnp.sum((position[None, :, None] >= ends_at[:, None, :]).astype(jnp.int32), axis=-1)).astype(jnp.int32)

def slot_ranks(route_ids, expert_count):
    one_hot = (route_ids[..., None] == jnp.arange(expert_count, dtype=jnp.int32)).astype(jnp.int32)
    earlier = jnp.cumsum(one_hot, axis=-2).astype(jnp.int32) - one_hot
    return lax.optimization_barrier(jnp.sum(earlier * one_hot, axis=-1)).astype(jnp.int32)

def relative_bias(rel_table, bucket_table, tok_rows):
    position = jnp.arange(tok_rows, dtype=jnp.int32)
    offset = (position[None, :] - position[:, None] + tok_rows).astype(jnp.int32)
    return jnp.transpose(jnp.take(rel_table, bucket_table, axis=0)[offset], (2, 0, 1))

def attend(query_heads, key_heads, value_heads, segment, pos_bias):
    scores = jnp.einsum('qhd,khd->hqk', query_heads, key_heads, precision=PRECISE) + pos_bias
    scores = low_back(scores)
    same_seq = segment[:, None] == segment[None, :]
    scores = jnp.where(same_seq[None], scores, MASKED)
    attn_weights = jax.nn.softmax(scores, axis=-1)
    return jnp.einsum('hqk,khd->qhd', low(attn_weights), value_heads, precision=PRECISE)

def expert_block(inputs):
    expert_rows, first_weight, second_weight = inputs
    hidden_pre = low_back(jnp.dot(expert_rows, first_weight, precision=PRECISE))
    return jnp.dot(low(jax.nn.gelu(hidden_pre)), second_weight, precision=PRECISE)

def reference(tokens, cotangent, seq_lengths, routes, bucket_table, w_query, w_key, w_value, w_output, w_router, norm_attn, norm_ffn, rel_bias, expert_in, expert_out):
    tok_rows = TOK_DEV
    segment = segment_table(seq_lengths, tok_rows)
    route_dev = routes[:, 0].reshape(RANKS, tok_rows)
    slot_rank = slot_ranks(route_dev, EXPERTS)
    rank_ids = jnp.arange(RANKS, dtype=jnp.int32)[:, None]
    slot_index = (route_dev * (RANKS * CAP) + rank_ids * CAP + slot_rank).reshape(-1).astype(jnp.int32)
    chosen = routes[:, 0][:, None] == jnp.arange(EXPERTS, dtype=jnp.int32)[None, :]
    head_shape = (RANKS, tok_rows, HEADS, HEAD_DIM)

    def forward(inputs_f, query_w, key_w, value_w, output_w, router_w, gain_attn, gain_ffn, rel_table, first_w, second_w):
        normed = low(rms_norm(inputs_f, gain_attn))
        query_all = low(low_back(jnp.dot(normed, query_w, precision=PRECISE)))
        key_all = low(low_back(jnp.dot(normed, key_w, precision=PRECISE)))
        value_all = low(low_back(jnp.dot(normed, value_w, precision=PRECISE)))
        pos_bias = relative_bias(rel_table, bucket_table, tok_rows)

        def block(parts):
            return attend(parts[0], parts[1], parts[2], parts[3], pos_bias)
        attended = lax.map(jax.checkpoint(block), (query_all.reshape(head_shape), key_all.reshape(head_shape), value_all.reshape(head_shape), segment))
        attended = low(low_back(attended.reshape(TOKENS, HEADS * HEAD_DIM)))
        residual = inputs_f + low_back(jnp.dot(attended, output_w, precision=PRECISE))
        ffn_in = low(rms_norm(residual, gain_ffn))
        router_p = jax.nn.softmax(jnp.dot(ffn_in, router_w, precision=PRECISE), axis=-1)
        gate_value = lax.optimization_barrier(jnp.sum(jnp.where(chosen, router_p, 0.0), axis=-1, keepdims=True))
        sent_rows = low_back(ffn_in)
        buffer_rows = jnp.zeros((EXPERTS * RANKS * CAP, D), jnp.float32).at[slot_index].set(sent_rows)
        returned = lax.map(jax.checkpoint(expert_block), (buffer_rows.reshape(EXPERTS, RANKS * CAP, D), first_w, second_w))
        returned = low(low_back(returned.reshape(EXPERTS * RANKS * CAP, D)))
        return residual + gate_value * returned[slot_index]
    float_args = (tokens.astype(jnp.float32), w_query.astype(jnp.float32), w_key.astype(jnp.float32), w_value.astype(jnp.float32), w_output.astype(jnp.float32), w_router.astype(jnp.float32), norm_attn.astype(jnp.float32), norm_ffn.astype(jnp.float32), rel_bias.astype(jnp.float32), expert_in.astype(jnp.float32), expert_out.astype(jnp.float32))
    layer_out, pull_back = jax.vjp(forward, *float_args)
    grads = pull_back(cotangent.astype(jnp.float32))
    return (layer_out.astype(jnp.bfloat16), grads[0].astype(jnp.bfloat16), grads[1], grads[2], grads[3], grads[4], grads[5], grads[6], grads[7], grads[8], grads[9], grads[10])
```

```python
import jax
import jax.numpy as jnp
from jax import lax
from jax.experimental import pallas as pl
from jax.experimental.pallas import tpu as pltpu
from jax.sharding import PartitionSpec as P

D = 768
HEADS = 12
HEAD_DIM = 64
PAIR = 2 * HEAD_DIM
BAND = 128

EPSILON = 1e-06
PRECISE = lax.Precision.HIGHEST
MASKED = -1e30
F32 = jnp.float32
LOW = jnp.bfloat16


def norm_parts(values, gain_vec):
    scale_row = lax.rsqrt(jnp.mean(values * values, axis=-1, keepdims=True) + EPSILON)
    unit_rows = values * scale_row
    return (unit_rows * gain_vec, unit_rows, scale_row)


def norm_back(grad_rows, unit_rows, scale_row, gain_vec):
    gain_grad = jnp.sum(grad_rows * unit_rows, axis=0)
    scaled = grad_rows * gain_vec
    return (
        scale_row * (scaled - unit_rows * jnp.mean(scaled * unit_rows, axis=-1, keepdims=True)),
        gain_grad,
    )


def dot_nt(a, b):
    return lax.dot_general(a, b, (((1,), (1,)), ((), ())), preferred_element_type=F32)


def dot_tn(a, b):
    return lax.dot_general(a, b, (((0,), (0,)), ((), ())), preferred_element_type=F32)


def dot_nn(a, b):
    return jnp.dot(a, b, preferred_element_type=F32)


def attend_kernel(q_ref, k_ref, v_ref, offs_ref, seg_col_ref, seg_row_ref, out_ref, attn_ref):
    rows = q_ref.shape[0]
    span = 2 * rows
    same_seq = seg_col_ref[...] == seg_row_ref[...]
    for h in range(2):
        cols = slice(h * HEAD_DIM, (h + 1) * HEAD_DIM)
        wide = jnp.broadcast_to(offs_ref[h], (BAND, span))
        wide = pltpu.roll(wide, 0, 1, stride=1, stride_axis=0)
        for b in range(rows // BAND):
            part = slice(b * BAND, (b + 1) * BAND)
            start = (span - b * BAND) % span
            if start + rows <= span:
                bias = wide[:, start : start + rows]
            else:
                bias = jnp.concatenate(
                    [wide[:, start:], wide[:, : start + rows - span]], axis=1
                )
            scores = dot_nt(q_ref[part, cols], k_ref[:, cols]) + bias
            scores = jnp.where(same_seq[part], scores, MASKED)
            top = jnp.max(scores, axis=-1, keepdims=True)
            raised = jnp.exp(scores - top)
            total = jnp.sum(raised, axis=-1, keepdims=True)
            attn = (raised * (1.0 / total)).astype(LOW)
            attn_ref[h, part, :] = attn
            out_ref[part, cols] = dot_nn(attn, v_ref[:, cols]).astype(LOW)


def attend(qkv, offs, segment):
    rows = qkv.shape[0]
    pairs = HEADS // 2
    block = (rows, PAIR)
    return pl.pallas_call(
        attend_kernel,
        grid=(pairs,),
        in_specs=[
            pl.BlockSpec(block, lambda p: (0, p)),
            pl.BlockSpec(block, lambda p: (0, pairs + p)),
            pl.BlockSpec(block, lambda p: (0, 2 * pairs + p)),
            pl.BlockSpec((2, 1, 2 * rows), lambda p: (p, 0, 0)),
            pl.BlockSpec((rows, 1), lambda p: (0, 0)),
            pl.BlockSpec((1, rows), lambda p: (0, 0)),
        ],
        out_specs=[
            pl.BlockSpec(block, lambda p: (0, p)),
            pl.BlockSpec((2, rows, rows), lambda p: (p, 0, 0)),
        ],
        out_shape=[
            jax.ShapeDtypeStruct((rows, HEADS * HEAD_DIM), LOW),
            jax.ShapeDtypeStruct((HEADS, rows, rows), LOW),
        ],
        compiler_params=pltpu.CompilerParams(vmem_limit_bytes=40 * 1024 * 1024),
        cost_estimate=pl.CostEstimate(
            flops=4 * HEADS * rows * rows * HEAD_DIM,
            bytes_accessed=4 * rows * HEADS * HEAD_DIM * 2 + HEADS * rows * rows * 2,
            transcendentals=HEADS * rows * rows,
        ),
    )(qkv, qkv, qkv, offs, segment[:, None], segment[None, :])


def attend_back_kernel(q_ref, k_ref, v_ref, go_ref, attn_ref, gq_ref, gk_ref, gv_ref, diag_ref):
    rows = q_ref.shape[0]
    span = 2 * rows
    bands = rows // BAND
    down = lax.broadcasted_iota(jnp.int32, (BAND, BAND), 0)
    upside = (down + lax.broadcasted_iota(jnp.int32, (BAND, BAND), 1) == BAND - 1).astype(F32)
    for h in range(2):
        cols = slice(h * HEAD_DIM, (h + 1) * HEAD_DIM)
        pieces = [None] * (span // BAND)
        grad_parts = []
        for b in range(bands):
            part = slice(b * BAND, (b + 1) * BAND)
            attn = attn_ref[h, part, :].astype(F32)
            grad_attn = dot_nt(go_ref[part, cols], v_ref[:, cols])
            mean = jnp.sum(attn * grad_attn, axis=-1, keepdims=True)
            grad = (attn * (grad_attn - mean)).astype(LOW)
            grad_parts.append(grad)
            gq_ref[part, cols] = dot_nn(grad, k_ref[:, cols]).astype(LOW)
            grad_f = grad.astype(F32)
            for c in range(bands):
                at = (c - b) % (span // BAND)
                piece = grad_f[:, c * BAND : (c + 1) * BAND]
                pieces[at] = piece if pieces[at] is None else pieces[at] + piece
        grads = jnp.concatenate(grad_parts, axis=0)
        gk_ref[:, cols] = dot_tn(grads, q_ref[:, cols]).astype(LOW)
        gv_ref[:, cols] = dot_tn(attn_ref[h], go_ref[:, cols]).astype(LOW)
        pieces = [jnp.zeros((BAND, BAND), F32) if x is None else x for x in pieces]
        wide = jnp.concatenate(pieces, axis=1)
        wide = jnp.dot(upside, wide, precision=PRECISE, preferred_element_type=F32)
        wide = pltpu.roll(wide, span - BAND + 1, 1, stride=1, stride_axis=0)
        diag_ref[h] = jnp.sum(wide, axis=0, keepdims=True)


def attend_back(qkv, grad_attended, attn_low):
    rows = qkv.shape[0]
    pairs = HEADS // 2
    block = (rows, PAIR)
    flat = jax.ShapeDtypeStruct((rows, HEADS * HEAD_DIM), LOW)
    return pl.pallas_call(
        attend_back_kernel,
        grid=(pairs,),
        in_specs=[
            pl.BlockSpec(block, lambda p: (0, p)),
            pl.BlockSpec(block, lambda p: (0, pairs + p)),
            pl.BlockSpec(block, lambda p: (0, 2 * pairs + p)),
            pl.BlockSpec(block, lambda p: (0, p)),
            pl.BlockSpec((2, rows, rows), lambda p: (p, 0, 0)),
        ],
        out_specs=[
            pl.BlockSpec(block, lambda p: (0, p)),
            pl.BlockSpec(block, lambda p: (0, p)),
            pl.BlockSpec(block, lambda p: (0, p)),
            pl.BlockSpec((2, 1, 2 * rows), lambda p: (p, 0, 0)),
        ],
        out_shape=[flat, flat, flat, jax.ShapeDtypeStruct((HEADS, 1, 2 * rows), F32)],
        compiler_params=pltpu.CompilerParams(vmem_limit_bytes=40 * 1024 * 1024),
        cost_estimate=pl.CostEstimate(
            flops=8 * HEADS * rows * rows * HEAD_DIM,
            bytes_accessed=7 * rows * HEADS * HEAD_DIM * 2 + HEADS * rows * rows * 2,
            transcendentals=0,
        ),
    )(qkv, qkv, qkv, grad_attended, attn_low)


def swap(rows, experts):
    return lax.all_to_all(
        rows.reshape(experts, -1, rows.shape[-1]), "dp", split_axis=0, concat_axis=0, tiled=True
    ).reshape(rows.shape)


def group_sum(grads):
    share = lax.psum_scatter(grads, "fsdp", scatter_dimension=0, tiled=True)
    return lax.psum(share, "dp").astype(F32)


def in_column(values, rows):
    flat = values.reshape(-1, 1)
    return jnp.pad(flat, ((0, rows - flat.shape[0]), (0, 0)))


def local(
    tokens,
    cotangent,
    seq_lengths,
    routes,
    bucket_table,
    w_query,
    w_key,
    w_value,
    w_output,
    w_router,
    norm_attn,
    norm_ffn,
    rel_bias,
    expert_in,
    expert_out,
):
    tok_rows = tokens.shape[0]
    experts = lax.axis_size("dp")
    groups = lax.axis_size("fsdp")
    capacity = 2 * tok_rows // experts
    slots = experts * capacity
    share = w_query.shape[0]
    buckets_own = rel_bias.shape[0]
    buckets = buckets_own * groups
    wide = HEADS * HEAD_DIM
    small = -(-(experts + 3) // 128) * 128
    pack = jnp.concatenate(
        [
            w_query,
            w_key,
            w_value,
            w_output,
            w_router,
            norm_attn[:, None],
            norm_ffn[:, None],
            in_column(rel_bias, share),
            jnp.zeros((share, small - experts - 3), LOW),
        ],
        axis=1,
    )
    packed = lax.all_gather(pack, "fsdp", axis=0, tiled=True)
    qkv_w = packed[:, : 3 * wide]
    output_w = packed[:, 3 * wide : 3 * wide + D]
    rest = packed[:, 3 * wide + D :]
    router_w = rest[:, :experts]
    gain_attn = rest[:, experts].astype(F32)
    gain_ffn = rest[:, experts + 1].astype(F32)
    rel_table = (
        rest[:, experts + 2]
        .reshape(groups, share)[:, : buckets_own * HEADS]
        .reshape(buckets, HEADS)
    )
    first_w = lax.all_gather(expert_in[0], "fsdp", axis=1, tiled=True)
    second_w = lax.all_gather(expert_out[0], "fsdp", axis=0, tiled=True)

    route_ids = routes[:, 0]
    position = jnp.arange(tok_rows, dtype=jnp.int32)
    chosen = (route_ids[:, None] == jnp.arange(experts, dtype=jnp.int32)[None, :]).astype(F32)
    lower_tri = (position[:, None] > position[None, :]).astype(LOW)
    earlier = dot_nn(lower_tri, chosen.astype(LOW))
    slot_rank = jnp.sum(earlier * chosen, axis=1).astype(jnp.int32)
    slot_index = route_ids * capacity + slot_rank
    slot_ids = jnp.arange(slots, dtype=jnp.int32)
    slot_hot = (slot_ids[:, None] == slot_index[None, :]).astype(LOW)
    cot_arrived = swap(dot_nn(slot_hot, cotangent).astype(LOW), experts)

    ends_at = jnp.cumsum(seq_lengths[0])
    segment = jnp.sum((position[:, None] >= ends_at[None, :]).astype(jnp.int32), axis=1)
    inputs_f = tokens.astype(F32)
    normed_f, unit_one, scale_one = norm_parts(inputs_f, gain_attn)
    normed = normed_f.astype(LOW)
    qkv = dot_nn(normed, qkv_w).astype(LOW)
    rolled = jnp.roll(bucket_table, -tok_rows)
    bucket_hot = rolled[None, :] == jnp.arange(buckets, dtype=jnp.int32)[:, None]
    offs = dot_tn(rel_table, bucket_hot.astype(LOW))[:, None, :]
    attended, attn_low = attend(qkv, offs, segment)
    residual = inputs_f + dot_nn(attended, output_w)
    ffn_f, unit_two, scale_two = norm_parts(residual, gain_ffn)
    ffn_in = ffn_f.astype(LOW)
    router_p = jax.nn.softmax(dot_nn(ffn_in, router_w), axis=-1)
    gate_value = jnp.sum(router_p * chosen, axis=-1, keepdims=True)
    arrived = swap(dot_nn(slot_hot, ffn_in).astype(LOW), experts)

    own = (jnp.arange(experts, dtype=jnp.int32) == lax.axis_index("dp")).astype(F32)[None, :]
    router_there = jax.nn.softmax(dot_nn(arrived, router_w), axis=-1)
    gate_there = jnp.sum(router_there * own, axis=-1, keepdims=True)
    cot_f = cot_arrived.astype(F32)
    grad_arrived = (gate_there * cot_f).astype(LOW)
    hidden_pre = dot_nn(arrived, first_w)
    hidden_f, pull_back = jax.vjp(jax.nn.gelu, hidden_pre)
    hidden_act = hidden_f.astype(LOW)
    expert_result = dot_nn(hidden_act, second_w).astype(LOW)
    grad_gate = jnp.sum(cot_f * expert_result.astype(F32), axis=-1, keepdims=True)
    grad_logits = router_there * (own - gate_there) * grad_gate
    grad_pre = pull_back(dot_nt(grad_arrived, second_w))[0].astype(LOW)
    grad_rows = dot_nt(grad_pre, first_w) + jnp.dot(
        grad_logits, router_w.astype(F32).T, precision=PRECISE
    )
    grad_back = swap(grad_rows.astype(LOW), experts)
    first_term = dot_tn(arrived, grad_pre).astype(LOW)
    second_term = dot_tn(hidden_act, grad_arrived).astype(LOW)
    grad_first = lax.psum_scatter(first_term, "fsdp", scatter_dimension=1, tiled=True)
    grad_second = lax.psum_scatter(second_term, "fsdp", scatter_dimension=0, tiled=True)
    grad_router_w = jnp.dot(arrived.astype(F32).T, grad_logits, precision=PRECISE)
    expert_result, grad_back = lax.optimization_barrier((expert_result, grad_back))
    returned = swap(expert_result, experts)

    grad_out = cotangent.astype(F32)
    grad_ffn_in = dot_tn(slot_hot, grad_back)
    grad_from_ffn, grad_gain_ffn = norm_back(grad_ffn_in, unit_two, scale_two, gain_ffn)
    grad_residual = grad_out + grad_from_ffn
    grad_att = grad_residual.astype(LOW)
    grad_attended = dot_nt(grad_att, output_w).astype(LOW)
    grad_q, grad_k, grad_v, diag = attend_back(qkv, grad_attended, attn_low)
    grad_output_w = dot_tn(attended, grad_att)
    grad_rel = dot_general_buckets(bucket_hot, diag[:, 0, :])
    grad_qkv = jnp.concatenate([grad_q, grad_k, grad_v], axis=1)
    grad_qkv_w = dot_tn(normed, grad_qkv)
    grad_normed = dot_nt(grad_qkv, qkv_w)
    grad_from_attn, grad_gain_attn = norm_back(grad_normed, unit_one, scale_one, gain_attn)
    grad_tokens = (grad_residual + grad_from_attn).astype(LOW)
    token_out = dot_tn(slot_hot, returned)
    layer_out = (residual + gate_value * token_out).astype(LOW)
    rel_rows = jnp.pad(
        grad_rel.reshape(groups, buckets_own * HEADS), ((0, 0), (0, share - buckets_own * HEADS))
    ).reshape(D, 1)
    summed = group_sum(
        jnp.concatenate(
            [
                grad_qkv_w.astype(LOW),
                grad_output_w.astype(LOW),
                grad_router_w.astype(LOW),
                grad_gain_attn.astype(LOW)[:, None],
                grad_gain_ffn.astype(LOW)[:, None],
                rel_rows.astype(LOW),
                jnp.zeros((D, small - experts - 3), LOW),
            ],
            axis=1,
        )
    )
    last = 3 * wide + D
    return (
        layer_out,
        grad_tokens,
        summed[:, :wide],
        summed[:, wide : 2 * wide],
        summed[:, 2 * wide : 3 * wide],
        summed[:, 3 * wide : last],
        summed[:, last : last + experts],
        summed[:, last + experts],
        summed[:, last + experts + 1],
        summed[: buckets_own * HEADS, last + experts + 2].reshape(buckets_own, HEADS),
        grad_first.astype(F32)[None],
        grad_second.astype(F32)[None],
    )


def dot_general_buckets(bucket_hot, diag):
    return lax.dot_general(
        bucket_hot.astype(F32), diag, (((1,), (1,)), ((), ())), precision=PRECISE
    )


def solution(mesh):
    placed = (
        P(("fsdp", "dp"), None),
        P(("fsdp", "dp"), None),
        P(("fsdp", "dp"), None),
        P(("fsdp", "dp"), None),
        P(),
        P("fsdp", None),
        P("fsdp", None),
        P("fsdp", None),
        P("fsdp", None),
        P("fsdp", None),
        P("fsdp"),
        P("fsdp"),
        P("fsdp", None),
        P("dp", None, "fsdp"),
        P("dp", "fsdp", None),
    )
    return jax.shard_map(
        local,
        mesh=mesh,
        in_specs=placed,
        out_specs=(
            P(("fsdp", "dp"), None),
            P(("fsdp", "dp"), None),
            P("fsdp", None),
            P("fsdp", None),
            P("fsdp", None),
            P("fsdp", None),
            P("fsdp", None),
            P("fsdp"),
            P("fsdp"),
            P("fsdp", None),
            P("dp", None, "fsdp"),
            P("dp", "fsdp", None),
        ),
        check_vma=False,
    )
```
